256 devices in a mesh: tile: 16 (over y, x_lo, core), fsdp: 16 (over z, x_hi).
Axes of the slice: x: 4 (x_hi: 2, x_lo: 2; x = x_hi * 2 + x_lo), y: 4, z: 8, core: 2. Of those that a mesh axis runs over, the one named last changes fastest.
Arguments:
- tiles_in: bfloat16 [512, 32, 32, 256], P(('tile', 'fsdp')), may hold values from -6 to 6
- first_weight: bfloat16 [512, 2304], P('fsdp'), may hold values from -0.125 to 0.125
- first_bias: float32 [512], replicated, may hold values from -3 to 3
- second_weight: bfloat16 [512, 4608], P('fsdp'), may hold values from -0.09375 to 0.09375
- second_bias: float32 [512], replicated, may hold values from -3 to 3
- side_links: int32 [512, 4, 3], P(('tile', 'fsdp')), may hold values from 0 to 511, as said below
- corner_links: int32 [512, 4, 3], P(('tile', 'fsdp')), may hold values from 0 to 511, as said below
Outputs:
- pooled: bfloat16 [512, 16, 16, 512], P(('tile', 'fsdp'))
The draws below stay inside these ranges and needn't reach their ends.
Inputs may be any that keep to these rules, and one draw needn't show every extreme that they name: `side_links`: the tile across side s (0 north, 1 east, 2 south, 3 west) of a tile lies on the device one step in that direction, with wrap, in the grid whose rows are the tile index and whose columns are the fsdp index; a tile id g lies on the device numbered g // 2 with the fsdp index fastest. The second entry is a side 0..3, the third a flag 0 or 1. `corner_links`: the tile at corner c (0 north-west, 1 north-east, 2 south-east, 3 south-west) lies on the diagonal device in that direction, with wrap, in the same grid; the second entry is a corner 0..3, the third is 1 where four or five tiles meet and 0 where three meet.
All inputs are finite; a program needn't handle non-finite values.
Results may differ from the reference program's by a relative error of at most 0.0031.
Values may be sent and summed in bfloat16 or wider, within the bound.
A program may use at most 384 MiB of HBM per device.

```python
import jax
import jax.numpy as jnp
from jax import lax

CIN = 256
COUT = 512
P_SIZE = 32
TILE_DEV = 2
TILES = 512
N_TILE = 16
N_FSDP = 16


def link_table(key, row_steps, col_steps, flag_top):
    tile_ids = jnp.arange(TILES, dtype=jnp.int32)
    device_id = tile_ids // TILE_DEV
    grid_row = device_id // N_FSDP
    grid_col = device_id % N_FSDP
    key_local, key_pick, key_flag = jax.random.split(key, 3)
    near_row = (grid_row[:, None] + jnp.array(row_steps, jnp.int32)[None, :]) % N_TILE
    near_col = (grid_col[:, None] + jnp.array(col_steps, jnp.int32)[None, :]) % N_FSDP
    local_tile = jax.random.randint(key_local, (TILES, 4), 0, TILE_DEV, dtype=jnp.int32)
    near_ids = (near_row * N_FSDP + near_col) * TILE_DEV + local_tile
    pick_index = jax.random.randint(key_pick, (TILES, 4), 0, 4, dtype=jnp.int32)
    flag_value = jax.random.randint(key_flag, (TILES, 4), 0, flag_top, dtype=jnp.int32)
    return (near_ids, pick_index, flag_value)


def draw_side_links(key, part):
    near_ids, pick_index, flag_value = link_table(jax.random.fold_in(key, 11), [-1, 0, 1, 0], [0, 1, 0, -1], 2)
    return jnp.stack([near_ids, pick_index, flag_value], axis=-1).astype(jnp.int32)


def draw_corner_links(key, part):
    near_ids, pick_index, flag_value = link_table(jax.random.fold_in(key, 23), [-1, -1, 1, 1], [-1, 1, 1, -1], 4)
    live_flag = jnp.where(flag_value > 0, 1, 0).astype(jnp.int32)
    return jnp.stack([near_ids, pick_index, live_flag], axis=-1).astype(jnp.int32)


def level_of(own_key, shape, cuts, least, largest):
    loudness = 1.0
    for dim, blocks in cuts:
        heights = jax.random.uniform(jax.random.fold_in(jax.random.fold_in(own_key, 6), dim), (blocks,), jnp.float32, least / len(cuts), largest / len(cuts))
        loudness = loudness * jnp.repeat(jnp.exp(heights), shape[dim] // blocks).reshape((-1,) + (1,) * (len(shape) - 1 - dim))
    return loudness


def gaussian(key, dims, spread, limit, shards=(), held_as=jnp.bfloat16):
    loudness = level_of(key, dims, shards, -0.22, 0.18) if shards else 1.0
    result = jax.random.normal(key, dims, jnp.float32) * spread * loudness
    return jnp.minimum(jnp.maximum(result, -limit), limit).astype(held_as)


def setup_inputs(seed: int = 0) -> dict:
    key_list = jax.random.split(jax.random.key(seed), 8)
    return {
        "tiles_in": gaussian(key_list[0], (TILES, P_SIZE, P_SIZE, CIN), 1.0, 6.0, ((0, 256),)),
        "first_weight": gaussian(key_list[1], (COUT, 9 * CIN), (9 * CIN) ** -0.5, 0.125, ((0, 16),)),
        "first_bias": gaussian(key_list[2], (COUT,), 0.5, 3.0, (), jnp.float32),
        "second_weight": gaussian(key_list[3], (COUT, 9 * COUT), (9 * COUT) ** -0.5, 0.09375, ((0, 16),)),
        "second_bias": gaussian(key_list[4], (COUT,), 0.5, 3.0, (), jnp.float32),
        "side_links": draw_side_links(jax.random.fold_in(key_list[7], 71), 0),
        "corner_links": draw_corner_links(jax.random.fold_in(key_list[7], 71), 0),
    }


def border_parts(field):
    strips = jnp.stack([field[:, 0, :, :], field[:, :, -1, :], field[:, -1, ::-1, :], field[:, ::-1, 0, :]], axis=1)
    corners = jnp.stack([field[:, 0, 0, :], field[:, 0, -1, :], field[:, -1, -1, :], field[:, -1, 0, :]], axis=1)
    return strips, corners


def assemble(field, side_halo, corner_halo):
    upper_row = jnp.concatenate([corner_halo[:, 0:1], side_halo[:, 0], corner_halo[:, 1:2]], axis=1)
    bottom = jnp.concatenate([corner_halo[:, 3:4], side_halo[:, 2, ::-1], corner_halo[:, 2:3]], axis=1)
    middle = jnp.concatenate([side_halo[:, 3, ::-1, None, :], field, side_halo[:, 1, :, None, :]], axis=2)
    return jnp.concatenate([upper_row[:, None], middle, bottom[:, None]], axis=1)


def surround(field, side_links, corner_links):
    strips, corners = border_parts(field)
    chosen = strips[side_links[..., 0], side_links[..., 1]]
    chosen = jnp.where(side_links[..., 2][..., None, None] == 1, chosen, chosen[:, :, ::-1])
    corner_halo = corners[corner_links[..., 0], corner_links[..., 1]]
    corner_halo = jnp.where(corner_links[..., 2][..., None] == 1, corner_halo, jnp.zeros_like(corner_halo))
    return assemble(field, chosen, corner_halo)


def convolve(padded, weight):
    edge_len = padded.shape[0] - 2
    channels = padded.shape[2]
    running = jnp.zeros((edge_len * edge_len, weight.shape[0]), jnp.float32)
    for row_step in range(3):
        for col_step in range(3):
            tap_index = 3 * row_step + col_step
            window = padded[row_step:row_step + edge_len, col_step:col_step + edge_len, :].reshape(edge_len * edge_len, channels)
            tap_weight = weight[:, tap_index * channels:(tap_index + 1) * channels]
            running = running + jnp.dot(window.astype(jnp.float32), tap_weight.astype(jnp.float32).T)
    return running.reshape(edge_len, edge_len, weight.shape[0])


def reference(tiles_in, first_weight, first_bias, second_weight, second_bias, side_links, corner_links):
    padded_first = surround(tiles_in, side_links, corner_links)

    def first_tile(padded):
        return jax.nn.gelu(convolve(padded, first_weight) + first_bias, approximate=False).astype(jnp.bfloat16)

    hidden = lax.map(first_tile, padded_first)
    padded_second = surround(hidden, side_links, corner_links)

    def second_tile(padded):
        act_full = jax.nn.gelu(convolve(padded, second_weight) + second_bias, approximate=False)
        half = act_full.shape[0] // 2
        return act_full.reshape(half, 2, half, 2, act_full.shape[2]).mean(axis=(1, 3)).astype(jnp.bfloat16)

    return lax.map(second_tile, padded_second)
```

```python
import functools

import jax
import jax.numpy as jnp
from jax import lax
from jax.experimental import pallas as pl
from jax.experimental.pallas import tpu as pltpu
from jax.sharding import PartitionSpec as P


MESH = pl.DeviceIdType.MESH
BF = jnp.bfloat16
F32 = jnp.float32
CIN, COUT = 256, 512
CW = 768
NU = 9
SENDS = 24 + 8 * NU
ROW_OF_UNIT = (0, 1, 2, 1, 1, 0, 0, 2, 2)


def mod(v, n):
    return lax.rem(v, n)


def gelu(x):
    return 0.5 * x * (1.0 + lax.erf(x * 0.7071067811865476))


def iota(shape, dim):
    return lax.broadcasted_iota(jnp.int32, shape, dim)


def hot(mask):
    return jnp.where(mask, 1.0, 0.0).astype(BF)


def mm_nt(a, b):
    return lax.dot_general(a, b, (((1,), (1,)), ((), ())), preferred_element_type=F32)


def mm(a, b):
    return jnp.dot(a, b, preferred_element_type=F32)


def kernel(
    tiles, w1, b1, w2, b2, side, corner, out,
    wbuf, xin, x1, x2, acc, strips, sel, csel, req_out, req_in, hs1, hc1, hb1, hs2, hc2, hb2,
    lsem, ssem, zssem, zsem, xsem, ysem, sibsem, rqsem, h1sem, h2sem,
):
    tile = lax.axis_index("tile")
    fs = lax.axis_index("fsdp")
    core = mod(tile, 2)
    xlo = mod(lax.div(tile, 2), 2)
    y = lax.div(tile, 4)
    z = lax.div(fs, 2)
    xhi = mod(fs, 2)
    x = xhi * 2 + xlo
    par = mod(y, 2)
    q = par * 2 + xlo

    def dev(xx, yy, cc, zz):
        return {"tile": (yy * 2 + mod(xx, 2)) * 2 + cc, "fsdp": zz * 2 + lax.div(xx, 2)}

    sib = dev(x, y, 1 - core, z)
    ups = dev(x, mod(y + 1, 4), core, z)
    downs = dev(x, mod(y + 3, 4), core, z)
    xdev = [dev(mod(x + k, 4), y, core, z) for k in (1, 2, 3)]
    zdev = [dev(x, y, core, mod(z + k, 8)) for k in (4, 3, 5, 2, 6, 1, 7)]
    no, so = mod(tile + 15, 16), mod(tile + 1, 16)
    ea, we = mod(fs + 1, 16), mod(fs + 15, 16)
    around = [(no, fs), (tile, ea), (so, fs), (tile, we), (no, we), (no, ea), (so, ea), (so, we)]
    around = [{"tile": a, "fsdp": b} for a, b in around]
    opp = (2, 3, 0, 1, 6, 7, 4, 5)

    barrier = pltpu.get_barrier_semaphore()
    partners = [sib, ups, downs] + xdev + zdev + around
    for p in partners:
        pl.semaphore_signal(barrier, inc=1, device_id=p, device_id_type=MESH)

    mine = pl.multiple_of(core * 16, 16)
    tcopy = pltpu.make_async_copy(tiles, xin, lsem.at[NU])
    lcopies = []
    zq, zr = lax.div(z, 4), mod(z, 4)
    for u in range(NU):
        if u < 3:
            src = w1.at[pl.ds(mine, 16), pl.ds(u * CW, CW)]
        else:
            src = w2.at[pl.ds(mine, 16), pl.ds(ROW_OF_UNIT[u] * 2 * CW + ((u + 1) % 2) * CW, CW)]
        lcopies.append(pltpu.make_async_copy(src, wbuf.at[u, core, xhi, zr, zq], lsem.at[u]))
    tcopy.start()

    def own_each(what):
        for u in range(NU):

            @pl.when(zr == mod(q + u, 4))
            def _():
                what(lcopies[u])

    own_each(lambda c: c.start())

    sends = []

    def copy(src, dst, sem, to, out_sem):
        return pltpu.make_async_remote_copy(
            src_ref=src, dst_ref=dst, send_sem=out_sem, recv_sem=sem, device_id=to, device_id_type=MESH
        )

    def send(src, dst, sem, to):
        c = copy(src, dst, sem, to, ssem.at[len(sends)])
        c.start()
        sends.append(c)

    def recv(dst, sem):
        copy(dst, dst, sem, sib, ssem.at[0]).wait_recv()

    lane = iota((8, 128), 1)
    for d in range(4):
        if d % 2 == 0:
            t = lane >> 5
            pos = lane & 31
        else:
            t = (lane >> 3) & 1
            pos = ((lane & 7) << 2) + ((lane >> 4) & 3)
        p = pos if d < 2 else 31 - pos
        rows = []
        for tt in range(2):
            lt = mod(side[tt, d, 0], 2)
            ls = side[tt, d, 1]
            fl = side[tt, d, 2]
            late = ls >= 2
            turn = jnp.logical_xor(fl != 1, late)
            qq = jnp.where(turn, 31 - p, p)
            straight = ls * 64 + lt * 32 + qq
            across = ls * 64 + lt * 8 + ((qq & 3) << 4) + (qq >> 2)
            rows.append(jnp.where(mod(ls, 2) == 0, straight, across))
        row = jnp.where(t == 0, rows[0], rows[1])
        req_out[d] = jnp.where(lane < 64, row, -1)
    for c in range(4):
        row = jnp.full((8, 128), -1, jnp.int32)
        for tt in range(2):
            lt = mod(corner[tt, c, 0], 2)
            lc = corner[tt, c, 1]
            low = jnp.where(lc >= 2, 128, 0)
            end = jnp.where(jnp.logical_or(lc == 1, lc == 2), 31, 0)
            cell = jnp.where(corner[tt, c, 2] == 1, low + lt * 32 + end, -1)
            row = jnp.where(lane == ((c + 2) % 4) * 16 + tt, cell, row)
        req_out[4 + c] = row

    own_each(lambda c: c.wait())
    pl.semaphore_wait(barrier, len(partners))

    for d in range(8):
        send(req_out.at[d], req_in.at[opp[d]], rqsem.at[opp[d]], around[d])

    u0 = mod(z + 4 - q, 4)

    def z_copies(i, u):
        ref = wbuf.at[u, core, xhi, zr, zq]
        return [copy(ref, ref, zsem.at[u, zq], to, zssem.at[i, k]) for k, to in enumerate(zdev)]

    def z_each(what):
        for i in range(3):
            u = u0 + 4 * i

            @pl.when(u < NU)
            def _():
                for c in z_copies(i, u):
                    what(c)

    def x_stage(u):
        m = mod(q + u, 4)
        for h in range(2):

            @pl.when(z != m + 4 * h)
            def _():
                recv(wbuf.at[u, core, xhi, m, h], zsem.at[u, h])

        ref = wbuf.at[u, core, xhi, m]
        for k in range(3):
            send(ref, ref, xsem.at[u, k], xdev[k])

    def y_stage(u):
        for k in range(3):
            xs = mod(x + 3 - k, 4)
            m = mod(par * 2 + mod(xs, 2) + u, 4)
            recv(wbuf.at[u, core, lax.div(xs, 2), m], xsem.at[u, k])
        for h, to in ((0, ups), (1, downs)):
            for i in range(2):
                ref = wbuf.at[u, core, h, mod(par * 2 + u + i, 4)]
                send(ref, ref, ysem.at[u, h, i], to)

    def s_stage(u):
        for h in range(2):
            for i in range(2):
                recv(wbuf.at[u, core, h, mod((1 - par) * 2 + u + i, 4)], ysem.at[u, h, i])
        ref = wbuf.at[u, core]
        send(ref, ref, sibsem.at[u], sib)

    def ready(u):
        recv(wbuf.at[u, 1 - core], sibsem.at[u])

    def weight(u):
        return jnp.transpose(wbuf[u], (3, 2, 1, 0, 4, 5)).reshape(COUT, CW)

    def send_halos(field, ch, hs, hc, hb, sem):
        base = iota((64, 512), 0)
        col = iota((64, 512), 1)
        want = ((base & 31) << 4) + ((base >> 5) << 3)
        north = mm(hot(col == want), field[1, pl.ds(1, 32)].reshape(512, ch))
        south = mm(hot(col == want + 7), field[4, pl.ds(1, 32)].reshape(512, ch))
        st = strips.at[:, pl.ds(0, ch)]
        st[pl.ds(0, 64)] = north.astype(BF)
        st[pl.ds(64, 64)] = field[pl.ds(1, 4), 32].reshape(64, ch)
        st[pl.ds(128, 64)] = south.astype(BF)
        st[pl.ds(192, 64)] = field[pl.ds(1, 4), 1].reshape(64, ch)
        have = st[...]
        landing = (
            hb.at[0, pl.ds(0, 4)], hb.at[2, pl.ds(0, 4)], hb.at[1, pl.ds(0, 4)], hb.at[3, pl.ds(0, 4)],
            hb.at[0, 4], hb.at[0, 5], hb.at[1, 5], hb.at[1, 4],
        )
        for d in range(4):
            got = lax.dot_general(sel[d], have, (((0,), (0,)), ((), ())), preferred_element_type=F32)
            hs[d] = got[0:64].astype(BF).reshape(4, 16, ch)
            send(hs.at[d], landing[opp[d]], sem.at[opp[d]], around[d])
        got = lax.dot_general(csel[...], have, (((0,), (0,)), ((), ())), preferred_element_type=F32)
        hc[...] = got[0:64].astype(BF).reshape(4, 16, ch)
        for c in range(4):
            send(hc.at[c], landing[opp[4 + c]], sem.at[opp[4 + c]], around[4 + c])
        return landing

    def take_halos(field, ch, hb, sem, landing):
        for d in range(8):
            recv(landing[d], sem.at[d])
        field[pl.ds(1, 4), 33] = hb[2, 0:4]
        field[pl.ds(1, 4), 0] = hb[3, 0:4]
        r = iota((544, 96), 0)
        c = iota((544, 96), 1)
        jj = r >> 4
        t = (r >> 3) & 1
        inner = (t << 5) + jj - 1
        want = jnp.where(jj == 0, 64 + t, jnp.where(jj == 33, 80 + t, inner))
        rr = iota((544, ch), 0) & 7
        for n, (to, frm, ih, shift) in enumerate(((0, 4, 0, 1), (5, 1, 7, 543))):
            placed = mm(hot(jnp.logical_and(c == want, (r & 7) == ih)), hb[n].reshape(96, ch))
            moved = pltpu.roll(field[frm].reshape(544, ch).astype(F32), shift, 0)
            field[to] = jnp.where(rr == ih, placed, moved).astype(BF).reshape(34, 16, ch)

    z_each(lambda c: c.start())

    tcopy.wait()
    row = iota((512, 512), 0)
    col = iota((512, 512), 1)
    turn_in = hot(col == ((row & 15) << 5) + (row >> 4))
    for il in range(4):
        part = xin[:, :, il].reshape(512, CIN)
        x1[1 + il, pl.ds(1, 32)] = mm(turn_in, part).astype(BF).reshape(32, 16, CIN)

    for d in range(8):
        recv(req_in.at[d], rqsem.at[d])
    own_row = iota((256, 128), 0)
    for d in range(4):
        sel[d] = hot(own_row == req_in[d][0:1])
    asked = jnp.maximum(jnp.maximum(req_in[4], req_in[5]), jnp.maximum(req_in[6], req_in[7]))
    csel[...] = hot(own_row == asked[0:1])

    land1 = send_halos(x1, CIN, hs1, hc1, hb1, h1sem)
    x_stage(0)
    x_stage(1)
    x_stage(2)
    x_stage(3)
    take_halos(x1, CIN, hb1, h1sem, land1)
    x_stage(4)
    y_stage(0)
    x_stage(5)
    y_stage(1)
    x_stage(6)
    y_stage(2)
    x_stage(7)
    x_stage(8)
    y_stage(3)
    s_stage(0)
    ready(0)

    def first(u, lo, hi):
        def body(il, carry):
            lhs = jnp.concatenate(
                [x1[il + u, pl.ds(b, 32)].reshape(512, CIN) for b in range(3)], axis=1
            )
            d = mm_nt(lhs, weight(u))
            if u == 0:
                acc[il] = d
            elif u == 1:
                acc[il] = acc[il] + d
            else:
                x2[1 + il, pl.ds(1, 32)] = gelu(acc[il] + d + b1[...]).astype(BF).reshape(32, 16, COUT)
            return carry

        lax.fori_loop(lo, hi, body, 0)

    first(0, 0, 2)
    s_stage(1)
    y_stage(4)
    first(0, 2, 4)
    ready(1)
    first(1, 0, 2)
    s_stage(2)
    y_stage(5)
    first(1, 2, 4)
    ready(2)
    first(2, 0, 2)
    s_stage(3)
    y_stage(6)
    first(2, 2, 4)
    s_stage(4)
    y_stage(7)
    land2 = send_halos(x2, COUT, hs2, hc2, hb2, h2sem)
    ready(3)

    INNER = pl.ds(16, 480)

    def taps(a, half, il, j0, nj):
        def window(b):
            return x2[il + a, pl.ds(j0 + b, nj)].reshape(nj * 16, COUT)

        if half == 0:
            return jnp.concatenate([window(0), window(1)[:, 0:256]], axis=1)
        return jnp.concatenate([window(1)[:, 256:512], window(2)], axis=1)

    def inner(u):
        a = ROW_OF_UNIT[u]
        half = (u + 1) % 2

        def body(il, carry):
            d = mm_nt(taps(a, half, il, 1, 30), weight(u))
            if u == 3:
                acc[il, INNER] = d
            else:
                acc[il, INNER] = acc[il, INNER] + d
            return carry

        lax.fori_loop(1 if a == 0 else 0, 3 if a == 2 else 4, body, 0)

    inner(3)
    s_stage(5)
    y_stage(8)
    ready(4)
    inner(4)
    s_stage(6)
    ready(5)
    inner(5)
    s_stage(7)
    ready(6)
    inner(6)
    s_stage(8)
    ready(7)
    inner(7)
    ready(8)
    inner(8)

    take_halos(x2, COUT, hb2, h2sem, land2)
    for a, il in ((0, 0), (2, 3)):
        total = acc[il, INNER]
        for u in range(3, NU):
            if ROW_OF_UNIT[u] == a:
                total = total + mm_nt(taps(a, (u + 1) % 2, il, 1, 30), weight(u))
        acc[il, INNER] = total
    ends = None
    for u in range(3, NU):
        a = ROW_OF_UNIT[u]
        half = (u + 1) % 2

        def column(j):
            def window(b):
                return x2[pl.ds(a, 4), j + b].reshape(64, COUT)

            if half == 0:
                return jnp.concatenate([window(0), window(1)[:, 0:256]], axis=1)
            return jnp.concatenate([window(1)[:, 256:512], window(2)], axis=1)

        d = mm_nt(jnp.concatenate([column(0), column(31)], axis=0), weight(u))
        ends = d if ends is None else ends + d
    for il in range(4):
        acc[il, pl.ds(0, 16)] = ends[il * 16 : il * 16 + 16]
        acc[il, pl.ds(496, 16)] = ends[64 + il * 16 : 80 + il * 16]

    row = iota((256, 256), 0)
    col = iota((256, 256), 1)
    turn_out = hot(col == ((row & 15) << 4) + (row >> 4))
    for half in range(2):
        act = gelu(acc[2 * half] + b2[...]) + gelu(acc[2 * half + 1] + b2[...])
        act = act.reshape(16, 2, 16, COUT)
        pooled = ((act[:, 0] + act[:, 1]) * 0.25).reshape(256, COUT).astype(BF)
        out[:, :, half] = mm(turn_out, pooled).astype(BF).reshape(2, 8, 16, COUT)

    for c in sends:
        c.wait_send()
    z_each(lambda c: c.wait_send())


def shards(tiles_in, first_weight, first_bias, second_weight, second_bias, side_links, corner_links):
    dma = pltpu.SemaphoreType.DMA
    anywhere = pl.BlockSpec(memory_space=pl.ANY)
    vmem = pl.BlockSpec(memory_space=pltpu.VMEM)
    smem = pl.BlockSpec(memory_space=pltpu.SMEM)
    out = pl.pallas_call(
        kernel,
        out_shape=jax.ShapeDtypeStruct((2, 8, 2, 16, COUT), BF),
        in_specs=[anywhere, anywhere, vmem, anywhere, vmem, smem, smem],
        out_specs=vmem,
        scratch_shapes=[
            pltpu.VMEM((NU, 2, 2, 4, 2, 16, CW), BF),
            pltpu.VMEM((2, 8, 4, 32, CIN), BF),
            pltpu.VMEM((6, 34, 16, CIN), BF),
            pltpu.VMEM((6, 34, 16, COUT), BF),
            pltpu.VMEM((4, 512, COUT), F32),
            pltpu.VMEM((256, COUT), BF),
            pltpu.VMEM((4, 256, 128), BF),
            pltpu.VMEM((256, 128), BF),
            pltpu.VMEM((8, 8, 128), jnp.int32),
            pltpu.VMEM((8, 8, 128), jnp.int32),
            pltpu.VMEM((4, 4, 16, CIN), BF),
            pltpu.VMEM((4, 16, CIN), BF),
            pltpu.VMEM((4, 6, 16, CIN), BF),
            pltpu.VMEM((4, 4, 16, COUT), BF),
            pltpu.VMEM((4, 16, COUT), BF),
            pltpu.VMEM((4, 6, 16, COUT), BF),
            dma((NU + 1,)),
            dma((SENDS,)),
            dma((3, 7)),
            dma((NU, 2)),
            dma((NU, 3)),
            dma((NU, 2, 2)),
            dma((NU,)),
            dma((8,)),
            dma((8,)),
            dma((8,)),
        ],
        compiler_params=pltpu.CompilerParams(
            collective_id=0, has_side_effects=True, vmem_limit_bytes=56 * 2**20
        ),
        name="level",
    )(
        tiles_in.reshape(2, 8, 4, 32, CIN),
        first_weight,
        first_bias.reshape(1, COUT),
        second_weight,
        second_bias.reshape(1, COUT),
        side_links,
        corner_links,
    )
    return out.reshape(2, 16, 16, COUT)


def solution(mesh):
    placed = (
        P(("tile", "fsdp"), None, None, None),
        P("fsdp", None),
        P(),
        P("fsdp", None),
        P(),
        P(("tile", "fsdp"), None, None),
        P(("tile", "fsdp"), None, None),
    )
    return jax.shard_map(
        shards,
        mesh=mesh,
        in_specs=placed,
        out_specs=P(("tile", "fsdp"), None, None, None),
        check_vma=False,
    )
```

```python
import functools

import jax
import jax.numpy as jnp
from jax import lax
from jax.experimental import pallas as pl
from jax.experimental.pallas import tpu as pltpu
from jax.sharding import PartitionSpec as P


MESH = pl.DeviceIdType.MESH
BF = jnp.bfloat16
F32 = jnp.float32
CIN, COUT = 256, 512
CW = 768
NU = 9
SENDS = 24 + 6 * NU
ROW_OF_UNIT = (0, 1, 2, 1, 1, 0, 0, 2, 2)


def mod(v, n):
    return lax.rem(v, n)


def gelu(x):
    return 0.5 * x * (1.0 + lax.erf(x * 0.7071067811865476))


def iota(shape, dim):
    return lax.broadcasted_iota(jnp.int32, shape, dim)


def hot(mask):
    return jnp.where(mask, 1.0, 0.0).astype(BF)


def turned(mask):
    return jnp.where(mask, 1.0, 0.0).T[0:64].astype(BF)


def mm_nt(a, b):
    return lax.dot_general(a, b, (((1,), (1,)), ((), ())), preferred_element_type=F32)


def mm(a, b):
    return jnp.dot(a, b, preferred_element_type=F32)


def kernel(
    tiles, w1, b1, w2, b2, side, corner, out,
    wbuf, xin, x1, x2, acc, strips, sel, csel, req_out, req_in, hs1, hc1, hb1, hs2, hc2, hb2,
    lsem, ssem, zssem, zsem, xsem, ysem, sibsem, rqsem, h1sem, h2sem,
):
    tile = lax.axis_index("tile")
    fs = lax.axis_index("fsdp")
    core = mod(tile, 2)
    xlo = mod(lax.div(tile, 2), 2)
    y = lax.div(tile, 4)
    z = lax.div(fs, 2)
    xhi = mod(fs, 2)
    x = xhi * 2 + xlo
    par = mod(y, 2)
    q = par * 2 + xlo

    def dev(xx, yy, cc, zz):
        return {"tile": (yy * 2 + mod(xx, 2)) * 2 + cc, "fsdp": zz * 2 + lax.div(xx, 2)}

    sib = dev(x, y, 1 - core, z)
    ups = dev(x, mod(y + 1, 4), core, z)
    downs = dev(x, mod(y + 3, 4), core, z)
    xdev = [dev(mod(x + k, 4), y, core, z) for k in (1, 2, 3)]
    zdev = [dev(x, y, core, mod(z + k, 8)) for k in (4, 3, 5, 2, 6, 1, 7)]
    no, so = mod(tile + 15, 16), mod(tile + 1, 16)
    ea, we = mod(fs + 1, 16), mod(fs + 15, 16)
    around = [(no, fs), (tile, ea), (so, fs), (tile, we), (no, we), (no, ea), (so, ea), (so, we)]
    around = [{"tile": a, "fsdp": b} for a, b in around]
    opp = (2, 3, 0, 1, 6, 7, 4, 5)

    barrier = pltpu.get_barrier_semaphore()
    partners = [sib, ups, downs] + xdev + zdev + around
    for p in partners:
        pl.semaphore_signal(barrier, inc=1, device_id=p, device_id_type=MESH)

    mine = pl.multiple_of(core * 16, 16)
    tcopy = pltpu.make_async_copy(tiles, xin, lsem.at[NU])
    lcopies = []
    zq, zr = lax.div(z, 4), mod(z, 4)
    for u in range(NU):
        if u < 3:
            src = w1.at[pl.ds(mine, 16), pl.ds(u * CW, CW)]
        else:
            src = w2.at[pl.ds(mine, 16), pl.ds(ROW_OF_UNIT[u] * 2 * CW + ((u + 1) % 2) * CW, CW)]
        lcopies.append(pltpu.make_async_copy(src, wbuf.at[u, core, xhi, zr, zq], lsem.at[u]))
    tcopy.start()

    def own_each(what):
        for u in range(NU):

            @pl.when(zr == mod(q + 2 * (u % 2), 4))
            def _():
                what(lcopies[u])

    own_each(lambda c: c.start())

    sends = []

    def copy(src, dst, sem, to, out_sem):
        return pltpu.make_async_remote_copy(
            src_ref=src, dst_ref=dst, send_sem=out_sem, recv_sem=sem, device_id=to, device_id_type=MESH
        )

    def send(src, dst, sem, to):
        c = copy(src, dst, sem, to, ssem.at[len(sends)])
        c.start()
        sends.append(c)

    def recv(dst, sem):
        copy(dst, dst, sem, sib, ssem.at[0]).wait_recv()

    lane = iota((8, 128), 1)
    for d in range(4):
        if d % 2 == 0:
            t = lane >> 5
            pos = lane & 31
        else:
            t = (lane >> 3) & 1
            pos = ((lane & 7) << 2) + ((lane >> 4) & 3)
        p = pos if d < 2 else 31 - pos
        rows = []
        for tt in range(2):
            lt = mod(side[0, tt, d], 2)
            ls = side[1, tt, d]
            fl = side[2, tt, d]
            late = ls >= 2
            turn = jnp.logical_xor(fl != 1, late)
            qq = jnp.where(turn, 31 - p, p)
            straight = ls * 64 + lt * 32 + qq
            across = ls * 64 + lt * 8 + ((qq & 3) << 4) + (qq >> 2)
            rows.append(jnp.where(mod(ls, 2) == 0, straight, across))
        row = jnp.where(t == 0, rows[0], rows[1])
        req_out[d] = jnp.where(lane < 64, row, -1)
    for c in range(4):
        row = jnp.full((8, 128), -1, jnp.int32)
        for tt in range(2):
            lt = mod(corner[0, tt, c], 2)
            lc = corner[1, tt, c]
            low = jnp.where(lc >= 2, 128, 0)
            end = jnp.where(jnp.logical_or(lc == 1, lc == 2), 31, 0)
            cell = jnp.where(corner[2, tt, c] == 1, low + lt * 32 + end, -1)
            row = jnp.where(lane == ((c + 2) % 4) * 16 + tt, cell, row)
        req_out[4 + c] = row

    own_each(lambda c: c.wait())
    pl.semaphore_wait(barrier, len(partners))

    for d in range(8):
        send(req_out.at[d], req_in.at[opp[d]], rqsem.at[opp[d]], around[d])

    turn = mod(zr + 4 - q, 4)
    odd = lax.div(turn, 2)

    def z_each(what, groups):
        for g in groups:
            u = 2 * g + odd

            @pl.when(jnp.logical_and(mod(turn, 2) == 0, u < NU))
            def _():
                ref = wbuf.at[u, core, xhi, zr, zq]
                for k, to in enumerate(zdev):
                    what(copy(ref, ref, zsem.at[u, zq], to, zssem.at[g, k]))

    def x_stage(u):
        m = mod(q + 2 * (u % 2), 4)
        for h in range(2):

            @pl.when(z != m + 4 * h)
            def _():
                recv(wbuf.at[u, core, xhi, m, h], zsem.at[u, h])

        ref = wbuf.at[u, core, xhi, m]
        for k in range(3):
            send(ref, ref, xsem.at[u, k], xdev[k])

    def y_stage(u):
        for k in range(3):
            xs = mod(x + 3 - k, 4)
            m = mod(par * 2 + mod(xs, 2) + 2 * (u % 2), 4)
            recv(wbuf.at[u, core, lax.div(xs, 2), m], xsem.at[u, k])
        for h, to in ((0, ups), (1, downs)):
            ref = wbuf.at[u, core, h, pl.ds(mod(par * 2 + 2 * (u % 2), 4), 2)]
            send(ref, ref, ysem.at[u, h], to)

    def s_stage(u):
        for h in range(2):
            recv(wbuf.at[u, core, h, pl.ds(mod((1 - par) * 2 + 2 * (u % 2), 4), 2)], ysem.at[u, h])
        ref = wbuf.at[u, core]
        send(ref, ref, sibsem.at[u], sib)

    def ready(u):
        recv(wbuf.at[u, 1 - core], sibsem.at[u])

    def weight(u):
        return jnp.transpose(wbuf[u], (3, 2, 1, 0, 4, 5)).reshape(COUT, CW)

    def send_halos(field, ch, hs, hc, hb, sem):
        base = iota((64, 512), 0)
        col = iota((64, 512), 1)
        want = ((base & 31) << 4) + ((base >> 5) << 3)
        north = mm(hot(col == want), field[1, pl.ds(1, 32)].reshape(512, ch))
        south = mm(hot(col == want + 7), field[4, pl.ds(1, 32)].reshape(512, ch))
        st = strips.at[:, pl.ds(0, ch)]
        st[pl.ds(0, 64)] = north.astype(BF)
        st[pl.ds(64, 64)] = field[pl.ds(1, 4), 32].reshape(64, ch)
        st[pl.ds(128, 64)] = south.astype(BF)
        st[pl.ds(192, 64)] = field[pl.ds(1, 4), 1].reshape(64, ch)
        have = st[...]
        landing = (
            hb.at[0, pl.ds(0, 4)], hb.at[2, pl.ds(0, 4)], hb.at[1, pl.ds(0, 4)], hb.at[3, pl.ds(0, 4)],
            hb.at[0, 4], hb.at[0, 5], hb.at[1, 5], hb.at[1, 4],
        )
        for d in range(4):
            got = mm(sel[d], have)
            hs[d] = got.astype(BF).reshape(4, 16, ch)
            send(hs.at[d], landing[opp[d]], sem.at[opp[d]], around[d])
        got = mm(csel[...], have)
        hc[...] = got.astype(BF).reshape(4, 16, ch)
        for c in range(4):
            send(hc.at[c], landing[opp[4 + c]], sem.at[opp[4 + c]], around[4 + c])
        return landing

    def take_halos(field, ch, hb, sem, landing):
        for d in range(8):
            recv(landing[d], sem.at[d])
        field[pl.ds(1, 4), 33] = hb[2, 0:4]
        field[pl.ds(1, 4), 0] = hb[3, 0:4]
        r = iota((544, 96), 0)
        c = iota((544, 96), 1)
        jj = r >> 4
        t = (r >> 3) & 1
        inner = (t << 5) + jj - 1
        want = jnp.where(jj == 0, 64 + t, jnp.where(jj == 33, 80 + t, inner))
        rr = iota((544, ch), 0) & 7
        for n, (to, frm, ih, shift) in enumerate(((0, 4, 0, 1), (5, 1, 7, 543))):
            placed = mm(hot(jnp.logical_and(c == want, (r & 7) == ih)), hb[n].reshape(96, ch))
            moved = pltpu.roll(field[frm].reshape(544, ch).astype(F32), shift, 0)
            field[to] = jnp.where(rr == ih, placed, moved).astype(BF).reshape(34, 16, ch)


    row = iota((512, 512), 0)
    col = iota((512, 512), 1)
    turn_in = hot(col == ((row & 15) << 5) + (row >> 4))
    z_each(lambda c: c.start(), (0,))
    tcopy.wait()
    for il in range(4):
        part = xin[:, :, il].reshape(512, CIN)
        x1[1 + il, pl.ds(1, 32)] = mm(turn_in, part).astype(BF).reshape(32, 16, CIN)
    z_each(lambda c: c.start(), (1,))

    for d in range(8):
        recv(req_in.at[d], rqsem.at[d])
    own_row = iota((256, 128), 0)
    for d in range(4):
        sel[d] = turned(own_row == req_in[d][0:1])
    asked = jnp.maximum(jnp.maximum(req_in[4], req_in[5]), jnp.maximum(req_in[6], req_in[7]))
    csel[...] = turned(own_row == asked[0:1])
    land1 = send_halos(x1, CIN, hs1, hc1, hb1, h1sem)

    def pass_on(k):
        if 0 <= k < NU:
            x_stage(k)
        if 0 <= k - 3 < NU:
            y_stage(k - 3)
        if 0 <= k - 6 < NU:
            s_stage(k - 6)

    pass_on(0)
    z_each(lambda c: c.start(), (2,))
    pass_on(1)
    z_each(lambda c: c.start(), (3,))
    pass_on(2)
    z_each(lambda c: c.start(), (4,))
    take_halos(x1, CIN, hb1, h1sem, land1)
    pass_on(3)
    pass_on(4)
    pass_on(5)
    pass_on(6)
    pass_on(7)
    ready(0)

    def first(u, lo, hi):
        def body(il, carry):
            lhs = jnp.concatenate(
                [x1[il + u, pl.ds(b, 32)].reshape(512, CIN) for b in range(3)], axis=1
            )
            d = mm_nt(lhs, weight(u))
            if u == 0:
                acc[il] = d
            elif u == 1:
                acc[il] = acc[il] + d
            else:
                x2[1 + il, pl.ds(1, 32)] = gelu(acc[il] + d + b1[...]).astype(BF).reshape(32, 16, COUT)
            return carry

        lax.fori_loop(lo, hi, body, 0)

    for u in range(3):
        first(u, 0, 4)
        pass_on(8 + u)
        if u < 2:
            ready(u + 1)
    land2 = send_halos(x2, COUT, hs2, hc2, hb2, h2sem)
    ready(3)

    INNER = pl.ds(16, 480)

    def taps(a, half, il, j0, nj):
        def window(b):
            return x2[il + a, pl.ds(j0 + b, nj)].reshape(nj * 16, COUT)

        if half == 0:
            return jnp.concatenate([window(0), window(1)[:, 0:256]], axis=1)
        return jnp.concatenate([window(1)[:, 256:512], window(2)], axis=1)

    def inner(u, lo, hi):
        a = ROW_OF_UNIT[u]
        half = (u + 1) % 2

        def body(il, carry):
            d = mm_nt(taps(a, half, il, 1, 30), weight(u))
            if u == 3:
                acc[il, INNER] = d
            else:
                acc[il, INNER] = acc[il, INNER] + d
            return carry

        lax.fori_loop(lo, hi, body, 0)

    def rest(units):
        ends = None
        for u in units:
            a = ROW_OF_UNIT[u]
            half = (u + 1) % 2

            def column(j):
                def window(b):
                    return x2[pl.ds(a, 4), j + b].reshape(64, COUT)

                if half == 0:
                    return jnp.concatenate([window(0), window(1)[:, 0:256]], axis=1)
                return jnp.concatenate([window(1)[:, 256:512], window(2)], axis=1)

            d = mm_nt(jnp.concatenate([column(0), column(31)], axis=0), weight(u))
            ends = d if ends is None else ends + d
            if a == 0:
                acc[0, INNER] = acc[0, INNER] + mm_nt(taps(a, half, 0, 1, 30), weight(u))
        for il in range(4):
            acc[il, pl.ds(0, 16)] = ends[il * 16 : il * 16 + 16]
            acc[il, pl.ds(496, 16)] = ends[64 + il * 16 : 80 + il * 16]

    def whole(u, lo, hi):
        def body(il, carry):
            acc[il] = acc[il] + mm_nt(taps(ROW_OF_UNIT[u], (u + 1) % 2, il, 0, 32), weight(u))
            return carry

        lax.fori_loop(lo, hi, body, 0)

    inner(3, 0, 4)
    pass_on(11)
    ready(4)
    inner(4, 0, 4)
    pass_on(12)
    ready(5)
    inner(5, 1, 4)
    pass_on(13)
    take_halos(x2, COUT, hb2, h2sem, land2)
    rest((3, 4, 5))
    ready(6)
    whole(6, 0, 4)
    pass_on(14)
    ready(7)
    whole(7, 0, 4)
    ready(8)

    row = iota((256, 256), 0)
    col = iota((256, 256), 1)
    turn_out = hot(col == ((row & 15) << 4) + (row >> 4))
    for half in range(2):
        act = None
        for il in (2 * half, 2 * half + 1):
            last = mm_nt(taps(2, 1, il, 0, 32), weight(8))
            part = gelu(acc[il] + last + b2[...])
            act = part if act is None else act + part
        act = act.reshape(16, 2, 16, COUT)
        pooled = ((act[:, 0] + act[:, 1]) * 0.25).reshape(256, COUT).astype(BF)
        out[:, :, half] = mm(turn_out, pooled).astype(BF).reshape(2, 8, 16, COUT)

    for c in sends:
        c.wait_send()
    z_each(lambda c: c.wait_send(), range(5))


def shards(tiles_in, first_weight, first_bias, second_weight, second_bias, side_links, corner_links):
    dma = pltpu.SemaphoreType.DMA
    anywhere = pl.BlockSpec(memory_space=pl.ANY)
    vmem = pl.BlockSpec(memory_space=pltpu.VMEM)
    smem = pl.BlockSpec(memory_space=pltpu.SMEM)
    out = pl.pallas_call(
        kernel,
        out_shape=jax.ShapeDtypeStruct((2, 8, 2, 16, COUT), BF),
        in_specs=[anywhere, anywhere, vmem, anywhere, vmem, smem, smem],
        out_specs=vmem,
        scratch_shapes=[
            pltpu.VMEM((NU, 2, 2, 4, 2, 16, CW), BF),
            pltpu.VMEM((2, 8, 4, 32, CIN), BF),
            pltpu.VMEM((6, 34, 16, CIN), BF),
            pltpu.VMEM((6, 34, 16, COUT), BF),
            pltpu.VMEM((4, 512, COUT), F32),
            pltpu.VMEM((256, COUT), BF),
            pltpu.VMEM((4, 64, 256), BF),
            pltpu.VMEM((64, 256), BF),
            pltpu.VMEM((8, 8, 128), jnp.int32),
            pltpu.VMEM((8, 8, 128), jnp.int32),
            pltpu.VMEM((4, 4, 16, CIN), BF),
            pltpu.VMEM((4, 16, CIN), BF),
            pltpu.VMEM((4, 6, 16, CIN), BF),
            pltpu.VMEM((4, 4, 16, COUT), BF),
            pltpu.VMEM((4, 16, COUT), BF),
            pltpu.VMEM((4, 6, 16, COUT), BF),
            dma((NU + 1,)),
            dma((SENDS,)),
            dma((5, 7)),
            dma((NU, 2)),
            dma((NU, 3)),
            dma((NU, 2)),
            dma((NU,)),
            dma((8,)),
            dma((8,)),
            dma((8,)),
        ],
        compiler_params=pltpu.CompilerParams(
            collective_id=0, has_side_effects=True, vmem_limit_bytes=56 * 2**20
        ),
        name="level",
    )(
        tiles_in.reshape(2, 8, 4, 32, CIN),
        first_weight,
        first_bias.reshape(1, COUT),
        second_weight,
        second_bias.reshape(1, COUT),
        jnp.transpose(side_links, (2, 0, 1)),
        jnp.transpose(corner_links, (2, 0, 1)),
    )
    return out.reshape(2, 16, 16, COUT)


def solution(mesh):
    placed = (
        P(("tile", "fsdp"), None, None, None),
        P("fsdp", None),
        P(),
        P("fsdp", None),
        P(),
        P(("tile", "fsdp"), None, None),
        P(("tile", "fsdp"), None, None),
    )
    return jax.shard_map(
        shards,
        mesh=mesh,
        in_specs=placed,
        out_specs=P(("tile", "fsdp"), None, None, None),
        check_vma=False,
    )
```

```python
import functools

import jax
import jax.numpy as jnp
from jax import lax
from jax.experimental import pallas as pl
from jax.experimental.pallas import tpu as pltpu
from jax.sharding import PartitionSpec as P


MESH = pl.DeviceIdType.MESH
BF = jnp.bfloat16
F32 = jnp.float32
CIN, COUT = 256, 512
CW = 768
NU = 9
SENDS = 24 + 6 * NU
ROW_OF_UNIT = (0, 1, 2, 1, 1, 0, 0, 2, 2)


def mod(v, n):
    return lax.rem(v, n)


def gelu(x):
    return 0.5 * x * (1.0 + lax.erf(x * 0.7071067811865476))


def iota(shape, dim):
    return lax.broadcasted_iota(jnp.int32, shape, dim)


def hot(mask):
    return jnp.where(mask, 1.0, 0.0).astype(BF)


def turned(mask):
    return jnp.where(mask, 1.0, 0.0).T[0:64].astype(BF)


def mm_nt(a, b):
    return lax.dot_general(a, b, (((1,), (1,)), ((), ())), preferred_element_type=F32)


def mm(a, b):
    return jnp.dot(a, b, preferred_element_type=F32)


def kernel(
    tiles, w1, b1, w2, b2, side, corner, out,
    wbuf, xin, x1, x2, acc, strips, sel, csel, req_out, req_in, hs1, hc1, hb1, hs2, hc2, hb2,
    lsem, ssem, zssem, zsem, xsem, ysem, sibsem, rqsem, h1sem, h2sem,
):
    tile = lax.axis_index("tile")
    fs = lax.axis_index("fsdp")
    core = mod(tile, 2)
    xlo = mod(lax.div(tile, 2), 2)
    y = lax.div(tile, 4)
    z = lax.div(fs, 2)
    xhi = mod(fs, 2)
    x = xhi * 2 + xlo
    par = mod(y, 2)
    q = par * 2 + xlo

    def dev(xx, yy, cc, zz):
        return {"tile": (yy * 2 + mod(xx, 2)) * 2 + cc, "fsdp": zz * 2 + lax.div(xx, 2)}

    sib = dev(x, y, 1 - core, z)
    ups = dev(x, mod(y + 1, 4), core, z)
    downs = dev(x, mod(y + 3, 4), core, z)
    xdev = [dev(mod(x + k, 4), y, core, z) for k in (1, 2, 3)]
    zdev = [dev(x, y, core, mod(z + k, 8)) for k in (4, 3, 5, 2, 6, 1, 7)]
    no, so = mod(tile + 15, 16), mod(tile + 1, 16)
    ea, we = mod(fs + 1, 16), mod(fs + 15, 16)
    around = [(no, fs), (tile, ea), (so, fs), (tile, we), (no, we), (no, ea), (so, ea), (so, we)]
    around = [{"tile": a, "fsdp": b} for a, b in around]
    opp = (2, 3, 0, 1, 6, 7, 4, 5)

    barrier = pltpu.get_barrier_semaphore()
    partners = [sib, ups, downs] + xdev + zdev + around
    for p in partners:
        pl.semaphore_signal(barrier, inc=1, device_id=p, device_id_type=MESH)

    mine = pl.multiple_of(core * 16, 16)
    tcopy = pltpu.make_async_copy(tiles, xin, lsem.at[NU])
    lcopies = []
    zq, zr = lax.div(z, 4), mod(z, 4)
    for u in range(NU):
        if u < 3:
            src = w1.at[pl.ds(mine, 16), pl.ds(u * CW, CW)]
        else:
            src = w2.at[pl.ds(mine, 16), pl.ds(ROW_OF_UNIT[u] * 2 * CW + ((u + 1) % 2) * CW, CW)]
        lcopies.append(pltpu.make_async_copy(src, wbuf.at[u, core, xhi, zr, zq], lsem.at[u]))
    tcopy.start()

    def own_each(what):
        for u in range(NU):

            @pl.when(zr == mod(q + 2 * (u % 2), 4))
            def _():
                what(lcopies[u])

    own_each(lambda c: c.start())

    sends = []

    def copy(src, dst, sem, to, out_sem):
        return pltpu.make_async_remote_copy(
            src_ref=src, dst_ref=dst, send_sem=out_sem, recv_sem=sem, device_id=to, device_id_type=MESH
        )

    def send(src, dst, sem, to):
        c = copy(src, dst, sem, to, ssem.at[len(sends)])
        c.start()
        sends.append(c)

    def recv(dst, sem):
        copy(dst, dst, sem, sib, ssem.at[0]).wait_recv()

    lane = iota((8, 128), 1)
    for d in range(4):
        if d % 2 == 0:
            t = lane >> 5
            pos = lane & 31
        else:
            t = (lane >> 3) & 1
            pos = ((lane & 7) << 2) + ((lane >> 4) & 3)
        p = pos if d < 2 else 31 - pos
        rows = []
        for tt in range(2):
            lt = mod(side[0, tt, d], 2)
            ls = side[1, tt, d]
            fl = side[2, tt, d]
            late = ls >= 2
            turn = jnp.logical_xor(fl != 1, late)
            qq = jnp.where(turn, 31 - p, p)
            straight = ls * 64 + lt * 32 + qq
            across = ls * 64 + lt * 8 + ((qq & 3) << 4) + (qq >> 2)
            rows.append(jnp.where(mod(ls, 2) == 0, straight, across))
        row = jnp.where(t == 0, rows[0], rows[1])
        req_out[d] = jnp.where(lane < 64, row, -1)
    for c in range(4):
        row = jnp.full((8, 128), -1, jnp.int32)
        for tt in range(2):
            lt = mod(corner[0, tt, c], 2)
            lc = corner[1, tt, c]
            low = jnp.where(lc >= 2, 128, 0)
            end = jnp.where(jnp.logical_or(lc == 1, lc == 2), 31, 0)
            cell = jnp.where(corner[2, tt, c] == 1, low + lt * 32 + end, -1)
            row = jnp.where(lane == ((c + 2) % 4) * 16 + tt, cell, row)
        req_out[4 + c] = row

    own_each(lambda c: c.wait())
    pl.semaphore_wait(barrier, len(partners))

    for d in range(8):
        send(req_out.at[d], req_in.at[opp[d]], rqsem.at[opp[d]], around[d])

    turn = mod(zr + 4 - q, 4)
    odd = lax.div(turn, 2)

    def z_each(what, groups):
        for g in groups:
            u = 2 * g + odd

            @pl.when(jnp.logical_and(mod(turn, 2) == 0, u < NU))
            def _():
                ref = wbuf.at[u, core, xhi, zr, zq]
                for k, to in enumerate(zdev):
                    what(copy(ref, ref, zsem.at[u, zq], to, zssem.at[g, k]))

    def x_stage(u):
        m = mod(q + 2 * (u % 2), 4)
        for h in range(2):

            @pl.when(z != m + 4 * h)
            def _():
                recv(wbuf.at[u, core, xhi, m, h], zsem.at[u, h])

        ref = wbuf.at[u, core, xhi, m]
        for k in range(3):
            send(ref, ref, xsem.at[u, k], xdev[k])

    def y_stage(u):
        for k in range(3):
            xs = mod(x + 3 - k, 4)
            m = mod(par * 2 + mod(xs, 2) + 2 * (u % 2), 4)
            recv(wbuf.at[u, core, lax.div(xs, 2), m], xsem.at[u, k])
        for h, to in ((0, ups), (1, downs)):
            ref = wbuf.at[u, core, h, pl.ds(mod(par * 2 + 2 * (u % 2), 4), 2)]
            send(ref, ref, ysem.at[u, h], to)

    def s_stage(u):
        for h in range(2):
            recv(wbuf.at[u, core, h, pl.ds(mod((1 - par) * 2 + 2 * (u % 2), 4), 2)], ysem.at[u, h])
        ref = wbuf.at[u, core]
        send(ref, ref, sibsem.at[u], sib)

    def ready(u):
        recv(wbuf.at[u, 1 - core], sibsem.at[u])

    def weight(u):
        return jnp.transpose(wbuf[u], (3, 2, 1, 0, 4, 5)).reshape(COUT, CW)

    def send_halos(field, ch, hs, hc, hb, sem):
        base = iota((64, 512), 0)
        col = iota((64, 512), 1)
        want = ((base & 31) << 4) + ((base >> 5) << 3)
        north = mm(hot(col == want), field[1, pl.ds(1, 32)].reshape(512, ch))
        south = mm(hot(col == want + 7), field[4, pl.ds(1, 32)].reshape(512, ch))
        st = strips.at[:, pl.ds(0, ch)]
        st[pl.ds(0, 64)] = north.astype(BF)
        st[pl.ds(64, 64)] = field[pl.ds(1, 4), 32].reshape(64, ch)
        st[pl.ds(128, 64)] = south.astype(BF)
        st[pl.ds(192, 64)] = field[pl.ds(1, 4), 1].reshape(64, ch)
        have = st[...]
        landing = (
            hb.at[0, pl.ds(0, 4)], hb.at[2, pl.ds(0, 4)], hb.at[1, pl.ds(0, 4)], hb.at[3, pl.ds(0, 4)],
            hb.at[0, 4], hb.at[0, 5], hb.at[1, 5], hb.at[1, 4],
        )
        for d in range(4):
            got = mm(sel[d], have)
            hs[d] = got.astype(BF).reshape(4, 16, ch)
            send(hs.at[d], landing[opp[d]], sem.at[opp[d]], around[d])
        got = mm(csel[...], have)
        hc[...] = got.astype(BF).reshape(4, 16, ch)
        for c in range(4):
            send(hc.at[c], landing[opp[4 + c]], sem.at[opp[4 + c]], around[4 + c])
        return landing

    def take_halos(field, ch, hb, sem, landing):
        for d in range(8):
            recv(landing[d], sem.at[d])
        field[pl.ds(1, 4), 33] = hb[2, 0:4]
        field[pl.ds(1, 4), 0] = hb[3, 0:4]
        r = iota((544, 96), 0)
        c = iota((544, 96), 1)
        jj = r >> 4
        t = (r >> 3) & 1
        inner = (t << 5) + jj - 1
        want = jnp.where(jj == 0, 64 + t, jnp.where(jj == 33, 80 + t, inner))
        rr = iota((544, ch), 0) & 7
        for n, (to, frm, ih, shift) in enumerate(((0, 4, 0, 1), (5, 1, 7, 543))):
            placed = mm(hot(jnp.logical_and(c == want, (r & 7) == ih)), hb[n].reshape(96, ch))
            moved = pltpu.roll(field[frm].reshape(544, ch).astype(F32), shift, 0)
            field[to] = jnp.where(rr == ih, placed, moved).astype(BF).reshape(34, 16, ch)


    row = iota((512, 512), 0)
    col = iota((512, 512), 1)
    turn_in = hot(col == ((row & 15) << 5) + (row >> 4))
    z_each(lambda c: c.start(), (0,))
    tcopy.wait()
    for il in range(4):
        part = xin[:, :, il].reshape(512, CIN)
        x1[1 + il, pl.ds(1, 32)] = mm(turn_in, part).astype(BF).reshape(32, 16, CIN)
    z_each(lambda c: c.start(), (1,))

    for d in range(8):
        recv(req_in.at[d], rqsem.at[d])
    own_row = iota((256, 128), 0)
    for d in range(4):
        sel[d] = turned(own_row == req_in[d][0:1])
    asked = jnp.maximum(jnp.maximum(req_in[4], req_in[5]), jnp.maximum(req_in[6], req_in[7]))
    csel[...] = turned(own_row == asked[0:1])
    land1 = send_halos(x1, CIN, hs1, hc1, hb1, h1sem)

    def pass_on(k):
        if 0 <= k < NU:
            x_stage(k)
        if 0 <= k - 2 < NU:
            y_stage(k - 2)
        if 0 <= k - 5 < NU:
            s_stage(k - 5)

    pass_on(0)
    z_each(lambda c: c.start(), (2,))
    pass_on(1)
    z_each(lambda c: c.start(), (3,))
    pass_on(2)
    z_each(lambda c: c.start(), (4,))
    take_halos(x1, CIN, hb1, h1sem, land1)
    pass_on(3)
    pass_on(4)
    pass_on(5)
    pass_on(6)
    ready(0)

    def first(u, lo, hi):
        def body(il, carry):
            lhs = jnp.concatenate(
                [x1[il + u, pl.ds(b, 32)].reshape(512, CIN) for b in range(3)], axis=1
            )
            d = mm_nt(lhs, weight(u))
            if u == 0:
                acc[il] = d
            elif u == 1:
                acc[il] = acc[il] + d
            else:
                x2[1 + il, pl.ds(1, 32)] = gelu(acc[il] + d + b1[...]).astype(BF).reshape(32, 16, COUT)
            return carry

        lax.fori_loop(lo, hi, body, 0)

    for u in range(3):
        first(u, 0, 4)
        if u == 2:
            land2 = send_halos(x2, COUT, hs2, hc2, hb2, h2sem)
        pass_on(7 + u)
        ready(u + 1)

    INNER = pl.ds(16, 480)

    def taps(a, half, il, j0, nj):
        def window(b):
            return x2[il + a, pl.ds(j0 + b, nj)].reshape(nj * 16, COUT)

        if half == 0:
            return jnp.concatenate([window(0), window(1)[:, 0:256]], axis=1)
        return jnp.concatenate([window(1)[:, 256:512], window(2)], axis=1)

    def inner(u, lo, hi):
        a = ROW_OF_UNIT[u]
        half = (u + 1) % 2

        def body(il, carry):
            d = mm_nt(taps(a, half, il, 1, 30), weight(u))
            if u == 3:
                acc[il, INNER] = d
            else:
                acc[il, INNER] = acc[il, INNER] + d
            return carry

        lax.fori_loop(lo, hi, body, 0)

    def rest(units):
        ends = None
        for u in units:
            a = ROW_OF_UNIT[u]
            half = (u + 1) % 2

            def column(j):
                def window(b):
                    return x2[pl.ds(a, 4), j + b].reshape(64, COUT)

                if half == 0:
                    return jnp.concatenate([window(0), window(1)[:, 0:256]], axis=1)
                return jnp.concatenate([window(1)[:, 256:512], window(2)], axis=1)

            d = mm_nt(jnp.concatenate([column(0), column(31)], axis=0), weight(u))
            ends = d if ends is None else ends + d
            if a == 0:
                acc[0, INNER] = acc[0, INNER] + mm_nt(taps(a, half, 0, 1, 30), weight(u))
        for il in range(4):
            acc[il, pl.ds(0, 16)] = ends[il * 16 : il * 16 + 16]
            acc[il, pl.ds(496, 16)] = ends[64 + il * 16 : 80 + il * 16]

    def whole(u, lo, hi):
        def body(il, carry):
            acc[il] = acc[il] + mm_nt(taps(ROW_OF_UNIT[u], (u + 1) % 2, il, 0, 32), weight(u))
            return carry

        lax.fori_loop(lo, hi, body, 0)

    inner(3, 0, 4)
    pass_on(10)
    ready(4)
    inner(4, 0, 4)
    pass_on(11)
    ready(5)
    inner(5, 1, 4)
    pass_on(12)
    take_halos(x2, COUT, hb2, h2sem, land2)
    rest((3, 4, 5))
    ready(6)
    whole(6, 0, 4)
    pass_on(13)
    ready(7)
    whole(7, 0, 4)
    ready(8)

    row = iota((256, 256), 0)
    col = iota((256, 256), 1)
    turn_out = hot(col == ((row & 15) << 4) + (row >> 4))
    for half in range(2):
        act = None
        for il in (2 * half, 2 * half + 1):
            last = mm_nt(taps(2, 1, il, 0, 32), weight(8))
            part = gelu(acc[il] + last + b2[...])
            act = part if act is None else act + part
        act = act.reshape(16, 2, 16, COUT)
        pooled = ((act[:, 0] + act[:, 1]) * 0.25).reshape(256, COUT).astype(BF)
        out[:, :, half] = mm(turn_out, pooled).astype(BF).reshape(2, 8, 16, COUT)

    for c in sends:
        c.wait_send()
    z_each(lambda c: c.wait_send(), range(5))


def shards(tiles_in, first_weight, first_bias, second_weight, second_bias, side_links, corner_links):
    dma = pltpu.SemaphoreType.DMA
    anywhere = pl.BlockSpec(memory_space=pl.ANY)
    vmem = pl.BlockSpec(memory_space=pltpu.VMEM)
    smem = pl.BlockSpec(memory_space=pltpu.SMEM)
    out = pl.pallas_call(
        kernel,
        out_shape=jax.ShapeDtypeStruct((2, 8, 2, 16, COUT), BF),
        in_specs=[anywhere, anywhere, vmem, anywhere, vmem, smem, smem],
        out_specs=vmem,
        scratch_shapes=[
            pltpu.VMEM((NU, 2, 2, 4, 2, 16, CW), BF),
            pltpu.VMEM((2, 8, 4, 32, CIN), BF),
            pltpu.VMEM((6, 34, 16, CIN), BF),
            pltpu.VMEM((6, 34, 16, COUT), BF),
            pltpu.VMEM((4, 512, COUT), F32),
            pltpu.VMEM((256, COUT), BF),
            pltpu.VMEM((4, 64, 256), BF),
            pltpu.VMEM((64, 256), BF),
            pltpu.VMEM((8, 8, 128), jnp.int32),
            pltpu.VMEM((8, 8, 128), jnp.int32),
            pltpu.VMEM((4, 4, 16, CIN), BF),
            pltpu.VMEM((4, 16, CIN), BF),
            pltpu.VMEM((4, 6, 16, CIN), BF),
            pltpu.VMEM((4, 4, 16, COUT), BF),
            pltpu.VMEM((4, 16, COUT), BF),
            pltpu.VMEM((4, 6, 16, COUT), BF),
            dma((NU + 1,)),
            dma((SENDS,)),
            dma((5, 7)),
            dma((NU, 2)),
            dma((NU, 3)),
            dma((NU, 2)),
            dma((NU,)),
            dma((8,)),
            dma((8,)),
            dma((8,)),
        ],
        compiler_params=pltpu.CompilerParams(
            collective_id=0, has_side_effects=True, vmem_limit_bytes=56 * 2**20
        ),
        name="level",
    )(
        tiles_in.reshape(2, 8, 4, 32, CIN),
        first_weight,
        first_bias.reshape(1, COUT),
        second_weight,
        second_bias.reshape(1, COUT),
        jnp.transpose(side_links, (2, 0, 1)),
        jnp.transpose(corner_links, (2, 0, 1)),
    )
    return out.reshape(2, 16, 16, COUT)


def solution(mesh):
    placed = (
        P(("tile", "fsdp"), None, None, None),
        P("fsdp", None),
        P(),
        P("fsdp", None),
        P(),
        P(("tile", "fsdp"), None, None),
        P(("tile", "fsdp"), None, None),
    )
    return jax.shard_map(
        shards,
        mesh=mesh,
        in_specs=placed,
        out_specs=P(("tile", "fsdp"), None, None, None),
        check_vma=False,
    )
```

```python
import functools

import jax
import jax.numpy as jnp
from jax import lax
from jax.experimental import pallas as pl
from jax.experimental.pallas import tpu as pltpu
from jax.sharding import PartitionSpec as P


MESH = pl.DeviceIdType.MESH
BF = jnp.bfloat16
F32 = jnp.float32
CIN, COUT = 256, 512
CW = 768
NU = 9
SENDS = 24 + 6 * NU
ROW_OF_UNIT = (0, 1, 2, 1, 1, 0, 0, 2, 2)


def mod(v, n):
    return lax.rem(v, n)


def gelu(x):
    return 0.5 * x * (1.0 + lax.erf(x * 0.7071067811865476))


def iota(shape, dim):
    return lax.broadcasted_iota(jnp.int32, shape, dim)


def hot(mask):
    return jnp.where(mask, 1.0, 0.0).astype(BF)


def turned(mask):
    return jnp.where(mask, 1.0, 0.0).T[0:64].astype(BF)


def mm_nt(a, b):
    return lax.dot_general(a, b, (((1,), (1,)), ((), ())), preferred_element_type=F32)


def mm(a, b):
    return jnp.dot(a, b, preferred_element_type=F32)


def kernel(
    tiles, w1, b1, w2, b2, side, corner, out,
    wbuf, xin, x1, x2, acc, strips, sel, csel, req_out, req_in, hs1, hc1, hb1, hs2, hc2, hb2,
    lsem, ssem, zssem, zsem, xsem, ysem, sibsem, rqsem, h1sem, h2sem,
):
    tile = lax.axis_index("tile")
    fs = lax.axis_index("fsdp")
    core = mod(tile, 2)
    xlo = mod(lax.div(tile, 2), 2)
    y = lax.div(tile, 4)
    z = lax.div(fs, 2)
    xhi = mod(fs, 2)
    x = xhi * 2 + xlo
    par = mod(y, 2)
    q = par * 2 + xlo

    def dev(xx, yy, cc, zz):
        return {"tile": (yy * 2 + mod(xx, 2)) * 2 + cc, "fsdp": zz * 2 + lax.div(xx, 2)}

    sib = dev(x, y, 1 - core, z)
    ups = dev(x, mod(y + 1, 4), core, z)
    downs = dev(x, mod(y + 3, 4), core, z)
    xdev = [dev(mod(x + k, 4), y, core, z) for k in (1, 2, 3)]
    zdev = [dev(x, y, core, mod(z + k, 8)) for k in (4, 3, 5, 2, 6, 1, 7)]
    no, so = mod(tile + 15, 16), mod(tile + 1, 16)
    ea, we = mod(fs + 1, 16), mod(fs + 15, 16)
    around = [(no, fs), (tile, ea), (so, fs), (tile, we), (no, we), (no, ea), (so, ea), (so, we)]
    around = [{"tile": a, "fsdp": b} for a, b in around]
    opp = (2, 3, 0, 1, 6, 7, 4, 5)

    barrier = pltpu.get_barrier_semaphore()
    partners = [sib, ups, downs] + xdev + zdev + around
    for p in partners:
        pl.semaphore_signal(barrier, inc=1, device_id=p, device_id_type=MESH)

    mine = pl.multiple_of(core * 16, 16)
    tcopy = pltpu.make_async_copy(tiles, xin, lsem.at[NU])
    lcopies = []
    zq, zr = lax.div(z, 4), mod(z, 4)
    for u in range(NU):
        if u < 3:
            src = w1.at[pl.ds(mine, 16), pl.ds(u * CW, CW)]
        else:
            src = w2.at[pl.ds(mine, 16), pl.ds(ROW_OF_UNIT[u] * 2 * CW + ((u + 1) % 2) * CW, CW)]
        lcopies.append(pltpu.make_async_copy(src, wbuf.at[u, core, xhi, zr, zq], lsem.at[u]))
    tcopy.start()

    def own_each(what):
        for u in range(NU):

            @pl.when(zr == mod(q + 2 * (u % 2), 4))
            def _():
                what(lcopies[u])

    own_each(lambda c: c.start())

    sends = []

    def copy(src, dst, sem, to, out_sem):
        return pltpu.make_async_remote_copy(
            src_ref=src, dst_ref=dst, send_sem=out_sem, recv_sem=sem, device_id=to, device_id_type=MESH
        )

    def send(src, dst, sem, to):
        c = copy(src, dst, sem, to, ssem.at[len(sends)])
        c.start()
        sends.append(c)

    def recv(dst, sem):
        copy(dst, dst, sem, sib, ssem.at[0]).wait_recv()

    lane = iota((8, 128), 1)
    for d in range(4):
        if d % 2 == 0:
            t = lane >> 5
            pos = lane & 31
        else:
            t = (lane >> 3) & 1
            pos = ((lane & 7) << 2) + ((lane >> 4) & 3)
        p = pos if d < 2 else 31 - pos
        rows = []
        for tt in range(2):
            lt = mod(side[0, tt, d], 2)
            ls = side[1, tt, d]
            fl = side[2, tt, d]
            late = ls >= 2
            turn = jnp.logical_xor(fl != 1, late)
            qq = jnp.where(turn, 31 - p, p)
            straight = ls * 64 + lt * 32 + qq
            across = ls * 64 + lt * 8 + ((qq & 3) << 4) + (qq >> 2)
            rows.append(jnp.where(mod(ls, 2) == 0, straight, across))
        row = jnp.where(t == 0, rows[0], rows[1])
        req_out[d] = jnp.where(lane < 64, row, -1)
    for c in range(4):
        row = jnp.full((8, 128), -1, jnp.int32)
        for tt in range(2):
            lt = mod(corner[0, tt, c], 2)
            lc = corner[1, tt, c]
            low = jnp.where(lc >= 2, 128, 0)
            end = jnp.where(jnp.logical_or(lc == 1, lc == 2), 31, 0)
            cell = jnp.where(corner[2, tt, c] == 1, low + lt * 32 + end, -1)
            row = jnp.where(lane == ((c + 2) % 4) * 16 + tt, cell, row)
        req_out[4 + c] = row

    own_each(lambda c: c.wait())
    pl.semaphore_wait(barrier, len(partners))

    for d in range(8):
        send(req_out.at[d], req_in.at[opp[d]], rqsem.at[opp[d]], around[d])

    turn = mod(zr + 4 - q, 4)
    odd = lax.div(turn, 2)

    def z_each(what, groups):
        for g in groups:
            u = 2 * g + odd

            @pl.when(jnp.logical_and(mod(turn, 2) == 0, u < NU))
            def _():
                ref = wbuf.at[u, core, xhi, zr, zq]
                for k, to in enumerate(zdev):
                    what(copy(ref, ref, zsem.at[u, zq], to, zssem.at[g, k]))

    def x_stage(u):
        m = mod(q + 2 * (u % 2), 4)
        for h in range(2):

            @pl.when(z != m + 4 * h)
            def _():
                recv(wbuf.at[u, core, xhi, m, h], zsem.at[u, h])

        ref = wbuf.at[u, core, xhi, m]
        for k in range(3):
            send(ref, ref, xsem.at[u, k], xdev[k])

    def y_stage(u):
        for k in range(3):
            xs = mod(x + 3 - k, 4)
            m = mod(par * 2 + mod(xs, 2) + 2 * (u % 2), 4)
            recv(wbuf.at[u, core, lax.div(xs, 2), m], xsem.at[u, k])
        for h, to in ((0, ups), (1, downs)):
            ref = wbuf.at[u, core, h, pl.ds(mod(par * 2 + 2 * (u % 2), 4), 2)]
            send(ref, ref, ysem.at[u, h], to)

    def s_stage(u):
        for h in range(2):
            recv(wbuf.at[u, core, h, pl.ds(mod((1 - par) * 2 + 2 * (u % 2), 4), 2)], ysem.at[u, h])
        ref = wbuf.at[u, core]
        send(ref, ref, sibsem.at[u], sib)

    def ready(u):
        recv(wbuf.at[u, 1 - core], sibsem.at[u])

    def weight(u):
        return jnp.transpose(wbuf[u], (3, 2, 1, 0, 4, 5)).reshape(COUT, CW)

    def send_halos(field, ch, hs, hc, hb, sem):
        base = iota((64, 512), 0)
        col = iota((64, 512), 1)
        want = ((base & 31) << 4) + ((base >> 5) << 3)
        north = mm(hot(col == want), field[1, pl.ds(1, 32)].reshape(512, ch))
        south = mm(hot(col == want + 7), field[4, pl.ds(1, 32)].reshape(512, ch))
        st = strips.at[:, pl.ds(0, ch)]
        st[pl.ds(0, 64)] = north.astype(BF)
        st[pl.ds(64, 64)] = field[pl.ds(1, 4), 32].reshape(64, ch)
        st[pl.ds(128, 64)] = south.astype(BF)
        st[pl.ds(192, 64)] = field[pl.ds(1, 4), 1].reshape(64, ch)
        have = st[...]
        landing = (
            hb.at[0, pl.ds(0, 4)], hb.at[2, pl.ds(0, 4)], hb.at[1, pl.ds(0, 4)], hb.at[3, pl.ds(0, 4)],
            hb.at[0, 4], hb.at[0, 5], hb.at[1, 5], hb.at[1, 4],
        )
        for d in range(4):
            got = mm(sel[d], have)
            hs[d] = got.astype(BF).reshape(4, 16, ch)
            send(hs.at[d], landing[opp[d]], sem.at[opp[d]], around[d])
        got = mm(csel[...], have)
        hc[...] = got.astype(BF).reshape(4, 16, ch)
        for c in range(4):
            send(hc.at[c], landing[opp[4 + c]], sem.at[opp[4 + c]], around[4 + c])
        return landing

    def take_halos(field, ch, hb, sem, landing):
        for d in range(8):
            recv(landing[d], sem.at[d])
        field[pl.ds(1, 4), 33] = hb[2, 0:4]
        field[pl.ds(1, 4), 0] = hb[3, 0:4]
        r = iota((544, 96), 0)
        c = iota((544, 96), 1)
        jj = r >> 4
        t = (r >> 3) & 1
        inner = (t << 5) + jj - 1
        want = jnp.where(jj == 0, 64 + t, jnp.where(jj == 33, 80 + t, inner))
        rr = iota((544, ch), 0) & 7
        for n, (to, frm, ih, shift) in enumerate(((0, 4, 0, 1), (5, 1, 7, 543))):
            placed = mm(hot(jnp.logical_and(c == want, (r & 7) == ih)), hb[n].reshape(96, ch))
            moved = pltpu.roll(field[frm].reshape(544, ch).astype(F32), shift, 0)
            field[to] = jnp.where(rr == ih, placed, moved).astype(BF).reshape(34, 16, ch)


    row = iota((512, 512), 0)
    col = iota((512, 512), 1)
    turn_in = hot(col == ((row & 15) << 5) + (row >> 4))
    z_each(lambda c: c.start(), (0,))
    tcopy.wait()
    for il in range(4):
        part = xin[:, :, il].reshape(512, CIN)
        x1[1 + il, pl.ds(1, 32)] = mm(turn_in, part).astype(BF).reshape(32, 16, CIN)
    z_each(lambda c: c.start(), (1,))

    for d in range(8):
        recv(req_in.at[d], rqsem.at[d])
    own_row = iota((256, 128), 0)
    for d in range(4):
        sel[d] = turned(own_row == req_in[d][0:1])
    asked = jnp.maximum(jnp.maximum(req_in[4], req_in[5]), jnp.maximum(req_in[6], req_in[7]))
    csel[...] = turned(own_row == asked[0:1])
    land1 = send_halos(x1, CIN, hs1, hc1, hb1, h1sem)

    def pass_on(k):
        if 0 <= k - 5 < NU:
            s_stage(k - 5)
        if 0 <= k < NU:
            x_stage(k)
        if 0 <= k - 2 < NU:
            y_stage(k - 2)

    pass_on(0)
    z_each(lambda c: c.start(), (2,))
    pass_on(1)
    z_each(lambda c: c.start(), (3,))
    pass_on(2)
    z_each(lambda c: c.start(), (4,))
    take_halos(x1, CIN, hb1, h1sem, land1)
    pass_on(3)
    pass_on(4)
    pass_on(5)
    pass_on(6)
    ready(0)

    def first(u, lo, hi):
        def body(il, carry):
            lhs = jnp.concatenate(
                [x1[il + u, pl.ds(b, 32)].reshape(512, CIN) for b in range(3)], axis=1
            )
            d = mm_nt(lhs, weight(u))
            if u == 0:
                acc[il] = d
            elif u == 1:
                acc[il] = acc[il] + d
            else:
                x2[1 + il, pl.ds(1, 32)] = gelu(acc[il] + d + b1[...]).astype(BF).reshape(32, 16, COUT)
            return carry

        lax.fori_loop(lo, hi, body, 0)

    for u in range(3):
        first(u, 0, 4)
        if u == 2:
            land2 = send_halos(x2, COUT, hs2, hc2, hb2, h2sem)
        pass_on(7 + u)
        ready(u + 1)

    INNER = pl.ds(16, 480)

    def taps(a, half, il, j0, nj):
        def window(b):
            return x2[il + a, pl.ds(j0 + b, nj)].reshape(nj * 16, COUT)

        if half == 0:
            return jnp.concatenate([window(0), window(1)[:, 0:256]], axis=1)
        return jnp.concatenate([window(1)[:, 256:512], window(2)], axis=1)

    def inner(u, lo, hi):
        a = ROW_OF_UNIT[u]
        half = (u + 1) % 2

        def body(il, carry):
            d = mm_nt(taps(a, half, il, 1, 30), weight(u))
            if u == 3:
                acc[il, INNER] = d
            else:
                acc[il, INNER] = acc[il, INNER] + d
            return carry

        lax.fori_loop(lo, hi, body, 0)

    def rest(units):
        ends = None
        for u in units:
            a = ROW_OF_UNIT[u]
            half = (u + 1) % 2

            def column(j):
                def window(b):
                    return x2[pl.ds(a, 4), j + b].reshape(64, COUT)

                if half == 0:
                    return jnp.concatenate([window(0), window(1)[:, 0:256]], axis=1)
                return jnp.concatenate([window(1)[:, 256:512], window(2)], axis=1)

            d = mm_nt(jnp.concatenate([column(0), column(31)], axis=0), weight(u))
            ends = d if ends is None else ends + d
            if a == 0:
                acc[0, INNER] = acc[0, INNER] + mm_nt(taps(a, half, 0, 1, 30), weight(u))
        for il in range(4):
            acc[il, pl.ds(0, 16)] = ends[il * 16 : il * 16 + 16]
            acc[il, pl.ds(496, 16)] = ends[64 + il * 16 : 80 + il * 16]

    def whole(u, lo, hi):
        def body(il, carry):
            acc[il] = acc[il] + mm_nt(taps(ROW_OF_UNIT[u], (u + 1) % 2, il, 0, 32), weight(u))
            return carry

        lax.fori_loop(lo, hi, body, 0)

    inner(3, 0, 4)
    pass_on(10)
    ready(4)
    inner(4, 0, 4)
    pass_on(11)
    ready(5)
    inner(5, 1, 4)
    pass_on(12)
    take_halos(x2, COUT, hb2, h2sem, land2)
    rest((3, 4, 5))
    ready(6)
    whole(6, 0, 4)
    pass_on(13)
    ready(7)
    whole(7, 0, 4)
    ready(8)

    row = iota((256, 256), 0)
    col = iota((256, 256), 1)
    turn_out = hot(col == ((row & 15) << 4) + (row >> 4))
    for half in range(2):
        act = None
        for il in (2 * half, 2 * half + 1):
            last = mm_nt(taps(2, 1, il, 0, 32), weight(8))
            part = gelu(acc[il] + last + b2[...])
            act = part if act is None else act + part
        act = act.reshape(16, 2, 16, COUT)
        pooled = ((act[:, 0] + act[:, 1]) * 0.25).reshape(256, COUT).astype(BF)
        out[:, :, half] = mm(turn_out, pooled).astype(BF).reshape(2, 8, 16, COUT)

    for c in sends:
        c.wait_send()
    z_each(lambda c: c.wait_send(), range(5))


def shards(tiles_in, first_weight, first_bias, second_weight, second_bias, side_links, corner_links):
    dma = pltpu.SemaphoreType.DMA
    anywhere = pl.BlockSpec(memory_space=pl.ANY)
    vmem = pl.BlockSpec(memory_space=pltpu.VMEM)
    smem = pl.BlockSpec(memory_space=pltpu.SMEM)
    out = pl.pallas_call(
        kernel,
        out_shape=jax.ShapeDtypeStruct((2, 8, 2, 16, COUT), BF),
        in_specs=[anywhere, anywhere, vmem, anywhere, vmem, smem, smem],
        out_specs=vmem,
        scratch_shapes=[
            pltpu.VMEM((NU, 2, 2, 4, 2, 16, CW), BF),
            pltpu.VMEM((2, 8, 4, 32, CIN), BF),
            pltpu.VMEM((6, 34, 16, CIN), BF),
            pltpu.VMEM((6, 34, 16, COUT), BF),
            pltpu.VMEM((4, 512, COUT), F32),
            pltpu.VMEM((256, COUT), BF),
            pltpu.VMEM((4, 64, 256), BF),
            pltpu.VMEM((64, 256), BF),
            pltpu.VMEM((8, 8, 128), jnp.int32),
            pltpu.VMEM((8, 8, 128), jnp.int32),
            pltpu.VMEM((4, 4, 16, CIN), BF),
            pltpu.VMEM((4, 16, CIN), BF),
            pltpu.VMEM((4, 6, 16, CIN), BF),
            pltpu.VMEM((4, 4, 16, COUT), BF),
            pltpu.VMEM((4, 16, COUT), BF),
            pltpu.VMEM((4, 6, 16, COUT), BF),
            dma((NU + 1,)),
            dma((SENDS,)),
            dma((5, 7)),
            dma((NU, 2)),
            dma((NU, 3)),
            dma((NU, 2)),
            dma((NU,)),
            dma((8,)),
            dma((8,)),
            dma((8,)),
        ],
        compiler_params=pltpu.CompilerParams(
            collective_id=0, has_side_effects=True, vmem_limit_bytes=56 * 2**20
        ),
        name="level",
    )(
        tiles_in.reshape(2, 8, 4, 32, CIN),
        first_weight,
        first_bias.reshape(1, COUT),
        second_weight,
        second_bias.reshape(1, COUT),
        jnp.transpose(side_links, (2, 0, 1)),
        jnp.transpose(corner_links, (2, 0, 1)),
    )
    return out.reshape(2, 16, 16, COUT)


def solution(mesh):
    placed = (
        P(("tile", "fsdp"), None, None, None),
        P("fsdp", None),
        P(),
        P("fsdp", None),
        P(),
        P(("tile", "fsdp"), None, None),
        P(("tile", "fsdp"), None, None),
    )
    return jax.shard_map(
        shards,
        mesh=mesh,
        in_specs=placed,
        out_specs=P(("tile", "fsdp"), None, None, None),
        check_vma=False,
    )
```
